32 devices in a mesh: row: 8 (over z, x), col: 4 (over y, core).
Axes of the slice: x: 2, y: 2, z: 4, core: 2. Of those that a mesh axis runs over, the one named last changes fastest.
Arguments:
- features: float32 [6144, 64], P('row'), may hold values from -6 to 6
- noise: float32 [6144], P('row'), may hold values from 0.1 to 1
- tile_map: int32 [48], replicated, may hold values from 0 to 47, each once
- panel_tile: int32 [1], replicated, may hold values from 0 to 35
Outputs:
- panel: float32 [6144, 128], P('row')
- trailing: float32 [6144, 6144], P('row', 'col')
The draws below stay inside these ranges and needn't reach their ends.
Inputs may be any that keep to these rules, and one draw needn't show every extreme that they name: `tile_map`: a permutation: every global tile 0 to 47 is held by exactly one slot.
All inputs are finite; a program needn't handle non-finite values.
Results may differ from the reference program's by a relative error of at most 0.0003.
Values sent between devices are 32-bit elements; how exact they have to be, the bound alone decides.
A program may use at most 64 MiB of HBM per device.

```python
import math
import jax
import jax.numpy as jnp
from jax import lax

TILE = 128
FEAT = 64
NT = 48
M = 6144


def block_scale(stream_key, dims, cuts, smallest, largest):
    level, own = 1.0, jax.random.fold_in(stream_key, 6)
    for position, parts in cuts:
        steps = jnp.exp(jax.random.uniform(jax.random.fold_in(own, position), (parts,), jnp.float32, smallest / len(cuts), largest / len(cuts)))
        level = level * jnp.repeat(steps, dims[position] // parts).reshape([-1 if axis == position else 1 for axis in range(len(dims))])
    return level


def gaussian(own_key, extent, width, most, cuts=(), held_as=jnp.bfloat16):
    result = jax.random.normal(own_key, extent, jnp.float32) * width
    if len(cuts) > 0:
        result = block_scale(own_key, extent, cuts, -0.22, 0.18) * result
    return jnp.clip(result, min=-most, max=most).astype(held_as)


def setup_inputs(seed: int = 0) -> dict:
    keys = jax.random.split(jax.random.key(seed), 5)
    features = gaussian(keys[0], (M, FEAT), 1.0, 6.0, ((0, 8),), jnp.float32)
    noise = jnp.clip(jnp.exp(math.log(1.0) - 2.3025851 * jax.random.uniform(keys[1], (M,), jnp.float32) ** block_scale(keys[1], (M,), ((0, 8),), -0.2, 0.2)), 0.1, 1.0)
    tile_map = jax.random.permutation(keys[2], NT).astype(jnp.int32)
    panel_tile = jax.random.randint(keys[3], (1,), 0, 3 * NT // 4).astype(jnp.int32)
    return dict(features=features, noise=noise, tile_map=tile_map, panel_tile=panel_tile)


HIGHEST_MODE = lax.Precision.HIGHEST

def kernel_block(left_rows, right_rows):
    inner_part = jnp.dot(left_rows.astype(jnp.float32), right_rows.T.astype(jnp.float32), precision=HIGHEST_MODE, preferred_element_type=jnp.float32)
    left_sq = jnp.sum(left_rows * left_rows, axis=1)
    right_sq = jnp.sum(right_rows * right_rows, axis=1)
    return jnp.exp((2.0 * inner_part - left_sq[:, None] - right_sq[None, :]) / left_rows.shape[1])

def pivot_inverse(pivot_feat, pivot_noise):
    kernel_part = kernel_block(pivot_feat, pivot_feat) + jnp.diag(pivot_noise)
    lower_factor = jnp.linalg.cholesky(kernel_part)
    identity = jnp.eye(kernel_part.shape[0], dtype=kernel_part.dtype)
    return jax.scipy.linalg.solve_triangular(lower_factor, identity, lower=True)

def panel_piece(feat_rows, noise_rows, tile_of_row, offset_of_row, pivot_feat, inverse, pivot_tile):
    tile_width = pivot_feat.shape[0]
    kernel_part = kernel_block(feat_rows, pivot_feat)
    on_diagonal = (tile_of_row == pivot_tile)[:, None] & (offset_of_row[:, None] == jnp.arange(tile_width, dtype=jnp.int32)[None, :])
    kernel_part = kernel_part + jnp.where(on_diagonal, noise_rows[:, None], 0.0)
    factor = jnp.dot(kernel_part.astype(jnp.float32), inverse.T.astype(jnp.float32), precision=HIGHEST_MODE, preferred_element_type=jnp.float32)
    return jnp.where((tile_of_row >= pivot_tile)[:, None], factor, 0.0)

def trailing_block(row_feat, row_noise, row_panel, row_tile, row_offset, col_feat, col_panel, col_tile, col_offset, pivot_tile):
    kernel_part = kernel_block(row_feat, col_feat)
    same_entry = (row_tile[:, None] == col_tile[None, :]) & (row_offset[:, None] == col_offset[None, :])
    kernel_part = kernel_part + jnp.where(same_entry, row_noise[:, None], 0.0)
    kernel_part = kernel_part - jnp.dot(row_panel.astype(jnp.float32), col_panel.T.astype(jnp.float32), precision=HIGHEST_MODE, preferred_element_type=jnp.float32)
    live_entry = (row_tile[:, None] >= col_tile[None, :]) & (col_tile[None, :] > pivot_tile)
    return jnp.where(live_entry, kernel_part, 0.0)

def reference(features, noise, tile_map, panel_tile):
    tile_width = TILE
    pivot_tile = panel_tile[0]
    tile_count = tile_map.shape[0]
    slot_ids = jnp.arange(tile_count, dtype=jnp.int32)
    pivot_slot = jnp.sum(jnp.where(tile_map == pivot_tile, slot_ids, 0)).astype(jnp.int32)
    pivot_feat = lax.dynamic_slice_in_dim(features, pivot_slot * tile_width, tile_width, 0)
    pivot_noise = lax.dynamic_slice_in_dim(noise, pivot_slot * tile_width, tile_width, 0)
    inverse = pivot_inverse(pivot_feat, pivot_noise)
    tile_of_row = jnp.repeat(tile_map, tile_width)
    offset_of_row = jnp.tile(jnp.arange(tile_width, dtype=jnp.int32), tile_count)
    panel_rows = panel_piece(features, noise, tile_of_row, offset_of_row, pivot_feat, inverse, pivot_tile)

    def one_tile(slot_index):
        first_row = (slot_index * tile_width).astype(jnp.int32)
        row_feat = lax.dynamic_slice_in_dim(features, first_row, tile_width, 0)
        row_noise = lax.dynamic_slice_in_dim(noise, first_row, tile_width, 0)
        row_panel = lax.dynamic_slice_in_dim(panel_rows, first_row, tile_width, 0)
        row_tile = lax.dynamic_slice_in_dim(tile_of_row, first_row, tile_width, 0)
        row_offset = lax.dynamic_slice_in_dim(offset_of_row, first_row, tile_width, 0)
        return trailing_block(row_feat, row_noise, row_panel, row_tile, row_offset, features, panel_rows, tile_of_row, offset_of_row, pivot_tile)
    stacked = lax.map(one_tile, slot_ids)
    trailing = stacked.reshape(tile_count * tile_width, tile_count * tile_width)
    return (panel_rows, trailing)
```

```python
import functools

import jax
import jax.numpy as jnp
from jax import lax
from jax.experimental import pallas as pl
from jax.experimental.pallas import tpu as pltpu
from jax.sharding import PartitionSpec as P

TILE = 128
FEAT = 64
CAND = 72
DEPTH = 6 * FEAT + 16
BLOCK = 32
HIGHEST = lax.Precision.HIGHEST
MESH = pl.DeviceIdType.MESH
CONTRACT_FIRST = (((0,), (0,)), ((), ()))
CONTRACT_LAST = (((1,), (1,)), ((), ()))


def split3(x):
    hi = x.astype(jnp.bfloat16)
    rest = x - hi.astype(jnp.float32)
    mid = rest.astype(jnp.bfloat16)
    lo = (rest - mid.astype(jnp.float32)).astype(jnp.bfloat16)
    return hi, mid, lo


def norm_rows(f, first):
    sq = jnp.sum(f * f, axis=0, keepdims=True) * (-1.0 / FEAT)
    parts = [p.astype(jnp.float32) for p in split3(sq)]
    row = lax.broadcasted_iota(jnp.int32, (16, f.shape[1]), 0)
    out = jnp.zeros((16, f.shape[1]), jnp.float32)
    for k in range(3):
        out = jnp.where(row == first + k, parts[k], out)
        out = jnp.where(row == 3 - first + k, 1.0, out)
    return out.astype(jnp.bfloat16)


def left_terms(f):
    hi, mid, lo = split3(f * (2.0 / FEAT))
    return jnp.concatenate([hi, hi, mid, mid, hi, lo, norm_rows(f, 0)], axis=0)


def right_terms(f):
    hi, mid, lo = split3(f)
    return jnp.concatenate([hi, mid, hi, mid, lo, hi, norm_rows(f, 3)], axis=0)


def exponent(left, right):
    return lax.dot_general(left, right, CONTRACT_FIRST, preferred_element_type=jnp.float32)


def eliminate(table):
    lane = lax.broadcasted_iota(jnp.int32, (1, TILE), 1)
    done = []
    below = table
    for k in range(TILE // BLOCK):
        rows = below[:BLOCK]
        groups = [rows[g * 8 : g * 8 + 8] for g in range(BLOCK // 8)]
        sub = lax.broadcasted_iota(jnp.int32, (8, 1), 0)
        finished = []
        for j in range(BLOCK):
            at = k * BLOCK + j
            g, o = j // 8, j % 8
            row = groups[g][o : o + 1]
            pivot = row[:, at : at + 1]
            scaled = jnp.where(lane == at, 1.0, row) / pivot
            finished.append((row, pivot))
            for h in range(g, BLOCK // 8):
                col = groups[h][:, at : at + 1]
                if h == g:
                    col = jnp.where(sub > o, col, 0.0)
                    keep = (lane != at) | (sub <= o)
                else:
                    keep = lane != at
                groups[h] = jnp.where(keep, groups[h], 0.0) - col * scaled
        pieces = []
        for j in range(BLOCK):
            at = k * BLOCK + j
            row, pivot = finished[j]
            pieces.append(jnp.where(lane == at, 1.0, row) / jnp.sqrt(pivot))
        block = jnp.concatenate(pieces, axis=0)
        inverse_lane = lax.broadcasted_iota(jnp.int32, (BLOCK, TILE), 1)
        inverse_sub = lax.broadcasted_iota(jnp.int32, (BLOCK, TILE), 0) + k * BLOCK
        done.append(jnp.where(inverse_lane <= inverse_sub, block, 0.0))
        if (k + 1) * BLOCK < TILE:
            own = (lane >= k * BLOCK) & (lane < (k + 1) * BLOCK)
            right = jnp.where(
                (inverse_lane <= inverse_sub) | (inverse_lane >= (k + 1) * BLOCK), block, 0.0
            )
            update = lax.dot_general(
                block, right, CONTRACT_FIRST, precision=HIGHEST, preferred_element_type=jnp.float32
            )
            below = jnp.where(own, 0.0, below[BLOCK:]) - update[(k + 1) * BLOCK :]
    return jnp.concatenate(done, axis=0)


def gather_kernel(
    rows, per_col, tiles, map_ref, panel_ref, feat_ref, noise_ref, cand_ref, col_ref,
    own_ref, cand_send, cand_recv, col_send, col_recv, local_sem,
):
    r = lax.axis_index("row")
    c = lax.axis_index("col")
    barrier = pltpu.get_barrier_semaphore()
    for d in range(1, rows):
        pl.semaphore_signal(
            barrier, inc=1, device_id={"row": lax.rem(r + d, rows)}, device_id_type=MESH
        )
    feat = jnp.zeros((FEAT, TILE), jnp.float32)
    noise = jnp.zeros((1, TILE), jnp.float32)
    for s in range(tiles):
        held = map_ref[r * tiles + s] == panel_ref[0]
        feat = jnp.where(held, feat_ref[:, s * TILE : (s + 1) * TILE], feat)
        noise = jnp.where(held, noise_ref[s : s + 1, :], noise)
    own_ref[:FEAT] = feat
    own_ref[FEAT:] = jnp.broadcast_to(noise, (CAND - FEAT, TILE))
    pl.semaphore_wait(barrier, rows - 1)
    sends = []
    for d in range(1, rows):
        copy = pltpu.make_async_remote_copy(
            src_ref=own_ref, dst_ref=cand_ref.at[r],
            send_sem=cand_send.at[d], recv_sem=cand_recv.at[r],
            device_id={"row": lax.rem(r + d, rows)}, device_id_type=MESH,
        )
        copy.start()
        sends.append(copy)

    def col_copy(d, member):
        return pltpu.make_async_remote_copy(
            src_ref=feat_ref, dst_ref=col_ref.at[member],
            send_sem=col_send.at[d], recv_sem=col_recv.at[member],
            device_id={"row": lax.rem(r + d, rows)}, device_id_type=MESH,
        )

    member = lax.rem(r, per_col)
    is_source = r // per_col == c

    @pl.when(is_source)
    def _():
        for d in range(1, rows):
            col_copy(d, member).start()
        own = pltpu.make_async_copy(feat_ref, col_ref.at[member], local_sem)
        own.start()
        own.wait()

    mine = pltpu.make_async_copy(own_ref, cand_ref.at[r], local_sem)
    mine.start()
    mine.wait()
    for d in range(1, rows):
        source = lax.rem(r + d, rows)
        pltpu.make_async_remote_copy(
            src_ref=own_ref, dst_ref=cand_ref.at[source],
            send_sem=cand_send.at[d], recv_sem=cand_recv.at[source],
            device_id={"row": source}, device_id_type=MESH,
        ).wait_recv()
    for m in range(per_col):
        @pl.when(c * per_col + m != r)
        def _(m=m):
            col_copy(1, m).wait_recv()

    for copy in sends:
        copy.wait_send()

    @pl.when(is_source)
    def _():
        for d in range(1, rows):
            col_copy(d, member).wait_send()


def panel_kernel(
    tiles, per_col, slots, map_ref, panel_ref, feat_ref, noise_ref, cand_ref, col_ref,
    out_panel, out_trailing, inverse_ref, pivot_right, col_right, col_hi, col_lo,
):
    i = pl.program_id(0)
    r = lax.axis_index("row")
    c = lax.axis_index("col")
    pivot_tile = panel_ref[0]
    lane = lax.broadcasted_iota(jnp.int32, (TILE, TILE), 1)
    sub = lax.broadcasted_iota(jnp.int32, (TILE, TILE), 0)
    width = tiles * TILE

    @pl.when(i == 0)
    def _():
        owner = jnp.int32(0)
        for s in range(slots):
            owner += jnp.where(map_ref[s] == pivot_tile, s // tiles, 0)
        cand = cand_ref[owner]
        pivot = cand[:FEAT]
        pivot_noise = cand[FEAT : FEAT + 1]
        left = left_terms(pivot)
        right = right_terms(pivot)
        pivot_right[...] = right
        table = jnp.exp(exponent(left, right)) + jnp.where(lane == sub, pivot_noise, 0.0)
        inverse = eliminate(table)
        inverse_ref[...] = inverse
        for m in range(per_col):
            cols = pl.ds(m * width, width)
            col_right[:, cols] = right_terms(col_ref[m])
            kern = jnp.exp(exponent(left, col_right[:, cols]))
            panel = jnp.dot(inverse, kern, precision=HIGHEST, preferred_element_type=jnp.float32)
            hi = panel.astype(jnp.bfloat16)
            col_hi[:, cols] = hi
            col_lo[:, cols] = (panel - hi.astype(jnp.float32)).astype(jnp.bfloat16)

    here = map_ref[r * tiles + i]
    left = left_terms(feat_ref[:, pl.ds(pl.multiple_of(i * TILE, TILE), TILE)])
    noise = jnp.where(lane == sub, noise_ref[pl.ds(i, 1), :], 0.0)
    kern = jnp.exp(exponent(left, pivot_right[...])) + jnp.where(here == pivot_tile, noise, 0.0)
    panel = lax.dot_general(
        kern, inverse_ref[...], CONTRACT_LAST, precision=HIGHEST, preferred_element_type=jnp.float32
    )
    panel = jnp.where(here >= pivot_tile, panel, 0.0)
    out_panel[...] = panel
    hi = panel.astype(jnp.bfloat16)
    lo = (panel - hi.astype(jnp.float32)).astype(jnp.bfloat16)
    for t in range(0, per_col * tiles, 2):
        cols = pl.ds(t * TILE, 2 * TILE)
        kern = jnp.exp(exponent(left, col_right[:, cols]))
        ch, cl = col_hi[:, cols], col_lo[:, cols]
        prod = jnp.dot(
            jnp.concatenate([hi, hi, lo], axis=1), jnp.concatenate([ch, cl, ch], axis=0),
            preferred_element_type=jnp.float32,
        )
        value = kern - prod
        for u in range(2):
            there = map_ref[c * per_col * tiles + t + u]
            live = (here >= there) & (there > pivot_tile)
            part = value[:, u * TILE : (u + 1) * TILE] + jnp.where(here == there, noise, 0.0)
            out_trailing[:, (t + u) * TILE : (t + u + 1) * TILE] = jnp.where(live, part, 0.0)


def shards(features, noise, tile_map, panel_tile):
    width = features.shape[0]
    tiles = width // TILE
    rows = lax.axis_size("row")
    per_col = rows // lax.axis_size("col")
    slots = tile_map.shape[0]
    feat = features.T
    noise = noise.reshape(tiles, TILE)
    smem = pl.BlockSpec(memory_space=pltpu.SMEM)
    vmem = pl.BlockSpec(memory_space=pltpu.VMEM)
    cand, cols = pl.pallas_call(
        functools.partial(gather_kernel, rows, per_col, tiles),
        name="gather_features",
        out_shape=(
            jax.ShapeDtypeStruct((rows, CAND, TILE), jnp.float32),
            jax.ShapeDtypeStruct((per_col, FEAT, width), jnp.float32),
        ),
        in_specs=[smem, smem, vmem, vmem],
        out_specs=(vmem, vmem),
        scratch_shapes=[
            pltpu.VMEM((CAND, TILE), jnp.float32),
            pltpu.SemaphoreType.DMA((rows,)),
            pltpu.SemaphoreType.DMA((rows,)),
            pltpu.SemaphoreType.DMA((rows,)),
            pltpu.SemaphoreType.DMA((per_col,)),
            pltpu.SemaphoreType.DMA,
        ],
        compiler_params=pltpu.CompilerParams(
            collective_id=0, has_side_effects=True, vmem_limit_bytes=32 * 1024 * 1024
        ),
    )(tile_map, panel_tile, feat, noise)
    total = per_col * width
    return pl.pallas_call(
        functools.partial(panel_kernel, tiles, per_col, slots),
        name="panel_and_trailing",
        grid=(tiles,),
        out_shape=(
            jax.ShapeDtypeStruct((width, TILE), jnp.float32),
            jax.ShapeDtypeStruct((width, total), jnp.float32),
        ),
        in_specs=[smem, smem, vmem, vmem, vmem, vmem],
        out_specs=(
            pl.BlockSpec((TILE, TILE), lambda i: (i, 0)),
            pl.BlockSpec((TILE, total), lambda i: (i, 0)),
        ),
        scratch_shapes=[
            pltpu.VMEM((TILE, TILE), jnp.float32),
            pltpu.VMEM((DEPTH, TILE), jnp.bfloat16),
            pltpu.VMEM((DEPTH, total), jnp.bfloat16),
            pltpu.VMEM((TILE, total), jnp.bfloat16),
            pltpu.VMEM((TILE, total), jnp.bfloat16),
        ],
        compiler_params=pltpu.CompilerParams(vmem_limit_bytes=48 * 1024 * 1024),
    )(tile_map, panel_tile, feat, noise, cand, cols)


def solution(mesh):
    in_specs = (P("row", None), P("row"), P(), P())
    out_specs = (P("row", None), P("row", "col"))
    return jax.shard_map(shards, mesh=mesh, in_specs=in_specs, out_specs=out_specs, check_vma=False)
```

```python
import functools

import jax
import jax.numpy as jnp
from jax import lax
from jax.experimental import pallas as pl
from jax.experimental.pallas import tpu as pltpu
from jax.sharding import PartitionSpec as P

TILE = 128
FEAT = 64
CAND = 72
DEPTH = 6 * FEAT + 16
BLOCK = 32
HIGHEST = lax.Precision.HIGHEST
MESH = pl.DeviceIdType.MESH
CONTRACT_FIRST = (((0,), (0,)), ((), ()))
CONTRACT_LAST = (((1,), (1,)), ((), ()))


def split3(x):
    hi = x.astype(jnp.bfloat16)
    rest = x - hi.astype(jnp.float32)
    mid = rest.astype(jnp.bfloat16)
    lo = (rest - mid.astype(jnp.float32)).astype(jnp.bfloat16)
    return hi, mid, lo


def norm_rows(f, first):
    sq = jnp.sum(f * f, axis=0, keepdims=True) * (-1.0 / FEAT)
    parts = [p.astype(jnp.float32) for p in split3(sq)]
    row = lax.broadcasted_iota(jnp.int32, (16, f.shape[1]), 0)
    out = jnp.zeros((16, f.shape[1]), jnp.float32)
    for k in range(3):
        out = jnp.where(row == first + k, parts[k], out)
        out = jnp.where(row == 3 - first + k, 1.0, out)
    return out.astype(jnp.bfloat16)


def left_terms(f):
    hi, mid, lo = split3(f * (2.0 / FEAT))
    return jnp.concatenate([hi, hi, mid, mid, hi, lo, norm_rows(f, 0)], axis=0)


def right_terms(f):
    hi, mid, lo = split3(f)
    return jnp.concatenate([hi, mid, hi, mid, lo, hi, norm_rows(f, 3)], axis=0)


def exponent(left, right):
    return lax.dot_general(left, right, CONTRACT_FIRST, preferred_element_type=jnp.float32)


def eliminate(table, between=None):
    lane = lax.broadcasted_iota(jnp.int32, (1, TILE), 1)
    sub = lax.broadcasted_iota(jnp.int32, (8, 1), 0)
    block_lane = lax.broadcasted_iota(jnp.int32, (BLOCK, TILE), 1)
    block_sub = lax.broadcasted_iota(jnp.int32, (BLOCK, TILE), 0)
    done = []
    below = table
    for k in range(TILE // BLOCK):
        groups = [below[g * 8 : g * 8 + 8] for g in range(BLOCK // 8)]
        pieces = []
        for j in range(BLOCK):
            at = k * BLOCK + j
            g, o = j // 8, j % 8
            row = groups[g][o : o + 1]
            pivot = row[:, at : at + 1]
            unit = jnp.where(lane == at, 1.0, row)
            pieces.append(unit / jnp.sqrt(pivot))
            scaled = unit / pivot
            for h in range(g, BLOCK // 8):
                col = groups[h][:, at : at + 1]
                if h == g:
                    col = jnp.where(sub > o, col, 0.0)
                    keep = (lane != at) | (sub <= o)
                else:
                    keep = lane != at
                groups[h] = jnp.where(keep, groups[h], 0.0) - col * scaled
            if between is not None and j % 8 == 7:
                between(at // 8)
        block = jnp.concatenate(pieces, axis=0)
        lower = block_lane <= block_sub + k * BLOCK
        done.append(jnp.where(lower, block, 0.0))
        if (k + 1) * BLOCK < TILE:
            own = (lane >= k * BLOCK) & (lane < (k + 1) * BLOCK)
            right = jnp.where(lower | (block_lane >= (k + 1) * BLOCK), block, 0.0)
            update = lax.dot_general(
                block, right, CONTRACT_FIRST, precision=HIGHEST, preferred_element_type=jnp.float32
            )
            below = jnp.where(own, 0.0, below[BLOCK:]) - update[(k + 1) * BLOCK :]
    return jnp.concatenate(done, axis=0)


CHUNKS = 4


def gather_kernel(
    lines, across, cols, tiles, map_hbm, panel_hbm, feat_hbm, noise_hbm,
    left_out, noise_out, here_out, there_out, pivot_out, inverse_out, pleft_out, pright_out, col_ref,
    map_ref, panel_ref, feat_ref, own_ref, sum_ref, near_ref, far_ref,
    in_sem, near_send, near_recv, far_send, far_recv, line_send, line_recv, side_send, side_recv, local_sem,
):
    r = lax.axis_index("row")
    c = lax.axis_index("col")
    rows = lines * across
    per_col = rows // cols
    z = r // across
    x = lax.rem(r, across)
    loads = [
        pltpu.make_async_copy(src, dst, in_sem.at[n])
        for n, (src, dst) in enumerate(
            [(map_hbm, map_ref), (panel_hbm, panel_ref), (feat_hbm, feat_ref), (noise_hbm, noise_out)]
        )
    ]
    for load in loads:
        load.start()
    barrier = pltpu.get_barrier_semaphore()
    for d in range(1, rows):
        pl.semaphore_signal(
            barrier, inc=1, device_id={"row": lax.rem(r + d, rows)}, device_id_type=MESH
        )
    for load in loads:
        load.wait()
    pivot_tile = panel_ref[0]
    feat = jnp.zeros((FEAT, TILE), jnp.float32)
    noise = jnp.zeros((1, TILE), jnp.float32)
    for s in range(tiles):
        held = map_ref[r * tiles + s] == pivot_tile
        feat = jnp.where(held, feat_ref[:, s * TILE : (s + 1) * TILE], feat)
        noise = jnp.where(held, noise_out[s : s + 1, :], noise)
    own_ref[:FEAT] = feat
    own_ref[FEAT:] = jnp.broadcast_to(noise, (CAND - FEAT, TILE))
    pl.semaphore_wait(barrier, rows - 1)

    def near(d, src, dst):
        return pltpu.make_async_remote_copy(
            src_ref=own_ref, dst_ref=near_ref.at[d - 1],
            send_sem=near_send.at[d - 1], recv_sem=near_recv.at[d - 1],
            device_id={"row": z * across + lax.rem(x + d, across)}, device_id_type=MESH,
        )

    def far(d):
        return pltpu.make_async_remote_copy(
            src_ref=sum_ref, dst_ref=far_ref.at[d - 1],
            send_sem=far_send.at[d - 1], recv_sem=far_recv.at[d - 1],
            device_id={"row": lax.rem(z + d, lines) * across + x}, device_id_type=MESH,
        )

    nears = [near(d, None, None) for d in range(1, across)]
    fars = [far(d) for d in range(1, lines)]
    for copy in nears:
        copy.start()
    for s in range(tiles):
        left_out[:, s * TILE : (s + 1) * TILE] = left_terms(feat_ref[:, s * TILE : (s + 1) * TILE])
        here_out[s * 8 : s * 8 + 8] = jnp.full((8, TILE), map_ref[r * tiles + s], jnp.int32)
    for t in range(per_col * tiles):
        there_out[:, t * TILE : (t + 1) * TILE] = jnp.full(
            (8, TILE), map_ref[c * per_col * tiles + t], jnp.int32
        )
    pivot_out[...] = jnp.full((8, TILE), pivot_tile, jnp.int32)
    for copy in nears:
        copy.wait_recv()
    total = own_ref[...]
    for d in range(1, across):
        total += near_ref[d - 1]
    sum_ref[...] = total
    for copy in fars:
        copy.start()
    for copy in fars:
        copy.wait_recv()
    for d in range(1, lines):
        total += far_ref[d - 1]

    first = c * per_col
    source_z = first // across
    first_x = lax.rem(first, across)
    member = x - first_x
    on_line = (member >= 0) & (member < per_col)
    slot = jnp.clip(member, 0, per_col - 1)
    hop = jnp.abs(z - source_z)
    rows_each = FEAT // CHUNKS

    def chunk(q):
        return col_ref.at[slot, pl.ds(q * rows_each, rows_each)]

    def line_copy(q, side):
        to = jnp.clip(z + (1 if side == 0 else -1), 0, lines - 1)
        return pltpu.make_async_remote_copy(
            src_ref=chunk(q), dst_ref=chunk(q),
            send_sem=line_send.at[side, q], recv_sem=line_recv.at[q],
            device_id={"row": to * across + x}, device_id_type=MESH,
        )

    def side_copy(q, d):
        return pltpu.make_async_remote_copy(
            src_ref=chunk(q), dst_ref=chunk(q),
            send_sem=side_send.at[d - 1, q], recv_sem=side_recv.at[slot, q],
            device_id={"row": z * across + lax.rem(x + d, across)}, device_id_type=MESH,
        )

    up = on_line & (z >= source_z) & (z < lines - 1)
    down = on_line & (z <= source_z) & (z > 0)

    def pass_on(q):
        @pl.when(up)
        def _():
            line_copy(q, 0).start()

        @pl.when(down)
        def _():
            line_copy(q, 1).start()

        for d in range(1, across):
            side_copy(q, d).start()

    def point(p):
        for h in range(lines):
            q = p - 2 * h
            if 0 <= q < CHUNKS:
                @pl.when(on_line & (hop == h))
                def _(h=h, q=q):
                    if h > 0:
                        line_copy(q, 0).wait_recv()
                    pass_on(q)

    @pl.when(on_line & (hop == 0))
    def _():
        own = pltpu.make_async_copy(feat_ref, col_ref.at[slot], local_sem)
        own.start()
        own.wait()

    pivot = total[:FEAT]
    left = left_terms(pivot)
    right = right_terms(pivot)
    pleft_out[...] = left
    pright_out[...] = right
    point(0)
    point(1)
    eye = lax.broadcasted_iota(jnp.int32, (TILE, TILE), 1) == lax.broadcasted_iota(
        jnp.int32, (TILE, TILE), 0
    )
    table = jnp.exp(exponent(left, right)) + jnp.where(eye, total[FEAT : FEAT + 1], 0.0)
    inverse_out[...] = eliminate(table, lambda n: point(n + 2))
    for p in range(TILE // 8 + 2, CHUNKS + 2 * lines):
        point(p)
    for m in range(per_col):
        for q in range(CHUNKS):
            part = col_ref.at[m, pl.ds(q * rows_each, rows_each)]

            @pl.when(x != first_x + m)
            def _(m=m, q=q, part=part):
                pltpu.make_async_remote_copy(
                    src_ref=part, dst_ref=part, send_sem=side_send.at[0, q],
                    recv_sem=side_recv.at[m, q], device_id={"row": z * across + first_x + m},
                    device_id_type=MESH,
                ).wait_recv()
    for copy in nears + fars:
        copy.wait_send()
    for q in range(CHUNKS):
        @pl.when(up)
        def _(q=q):
            line_copy(q, 0).wait_send()

        @pl.when(down)
        def _(q=q):
            line_copy(q, 1).wait_send()

        @pl.when(on_line)
        def _(q=q):
            for d in range(1, across):
                side_copy(q, d).wait_send()


def panel_kernel(
    tiles, per_col, left_ref, noise_ref, here_ref, there_ref, pivot_ref, inverse_ref, pleft_ref,
    pright_ref, col_ref, out_panel, out_trailing, col_right, col_hi, col_lo,
):
    i = pl.program_id(0)
    lane = lax.broadcasted_iota(jnp.int32, (TILE, TILE), 1)
    sub = lax.broadcasted_iota(jnp.int32, (TILE, TILE), 0)
    width = tiles * TILE

    @pl.when(i == 0)
    def _():
        for m in range(per_col):
            cols = pl.ds(m * width, width)
            col_right[:, cols] = right_terms(col_ref[m])
            kern = jnp.exp(exponent(pleft_ref[...], col_right[:, cols]))
            panel = jnp.dot(
                inverse_ref[...], kern, precision=HIGHEST, preferred_element_type=jnp.float32
            )
            hi = panel.astype(jnp.bfloat16)
            col_hi[:, cols] = hi
            col_lo[:, cols] = (panel - hi.astype(jnp.float32)).astype(jnp.bfloat16)

    here = here_ref[pl.ds(pl.multiple_of(i * 8, 8), 1), :]
    pivot_tile = pivot_ref[0:1, :]
    left = left_ref[:, pl.ds(pl.multiple_of(i * TILE, TILE), TILE)]
    noise = jnp.where(lane == sub, noise_ref[pl.ds(i, 1), :], 0.0)
    kern = jnp.exp(exponent(left, pright_ref[...])) + jnp.where(here == pivot_tile, noise, 0.0)
    panel = lax.dot_general(
        kern, inverse_ref[...], CONTRACT_LAST, precision=HIGHEST, preferred_element_type=jnp.float32
    )
    panel = jnp.where(here >= pivot_tile, panel, 0.0)
    out_panel[...] = panel
    hi = panel.astype(jnp.bfloat16)
    lo = (panel - hi.astype(jnp.float32)).astype(jnp.bfloat16)
    row_terms = jnp.concatenate([hi, hi, lo], axis=1)
    for t in range(0, per_col * tiles, 2):
        cols = pl.ds(t * TILE, 2 * TILE)
        kern = jnp.exp(exponent(left, col_right[:, cols]))
        ch, cl = col_hi[:, cols], col_lo[:, cols]
        prod = jnp.dot(
            row_terms, jnp.concatenate([ch, cl, ch], axis=0), preferred_element_type=jnp.float32
        )
        value = kern - prod
        for u in range(2):
            there = there_ref[0:1, (t + u) * TILE : (t + u + 1) * TILE]
            live = (here >= there) & (there > pivot_tile)
            part = value[:, u * TILE : (u + 1) * TILE] + jnp.where(here == there, noise, 0.0)
            out_trailing[:, (t + u) * TILE : (t + u + 1) * TILE] = jnp.where(live, part, 0.0)


def shards(features, noise, tile_map, panel_tile):
    width = features.shape[0]
    tiles = width // TILE
    rows = lax.axis_size("row")
    cols = lax.axis_size("col")
    per_col = rows // cols
    across = 2 ** ((rows.bit_length() - 1) // 2)
    lines = rows // across
    slots = tile_map.shape[0]
    total = per_col * width
    hbm = pl.BlockSpec(memory_space=pltpu.HBM)
    vmem = pl.BlockSpec(memory_space=pltpu.VMEM)
    dma = pltpu.SemaphoreType.DMA
    f32, bf16, i32 = jnp.float32, jnp.bfloat16, jnp.int32
    shape = jax.ShapeDtypeStruct
    gathered = pl.pallas_call(
        functools.partial(gather_kernel, lines, across, cols, tiles),
        name="gather_and_factor",
        out_shape=(
            shape((DEPTH, width), bf16),
            shape((tiles, TILE), f32),
            shape((tiles * 8, TILE), i32),
            shape((8, total), i32),
            shape((8, TILE), i32),
            shape((TILE, TILE), f32),
            shape((DEPTH, TILE), bf16),
            shape((DEPTH, TILE), bf16),
            shape((per_col, FEAT, width), f32),
        ),
        in_specs=[hbm] * 4,
        out_specs=(vmem,) * 9,
        scratch_shapes=[
            pltpu.SMEM((slots,), i32),
            pltpu.SMEM((1,), i32),
            pltpu.VMEM((FEAT, width), f32),
            pltpu.VMEM((CAND, TILE), f32),
            pltpu.VMEM((CAND, TILE), f32),
            pltpu.VMEM((across - 1, CAND, TILE), f32),
            pltpu.VMEM((lines - 1, CAND, TILE), f32),
            dma((4,)),
            dma((across - 1,)),
            dma((across - 1,)),
            dma((lines - 1,)),
            dma((lines - 1,)),
            dma((2, CHUNKS)),
            dma((CHUNKS,)),
            dma((across - 1, CHUNKS)),
            dma((per_col, CHUNKS)),
            dma,
        ],
        compiler_params=pltpu.CompilerParams(
            collective_id=0, has_side_effects=True, vmem_limit_bytes=32 * 1024 * 1024
        ),
    )(tile_map, panel_tile, features.T, noise.reshape(tiles, TILE))
    return pl.pallas_call(
        functools.partial(panel_kernel, tiles, per_col),
        name="panel_and_trailing",
        grid=(tiles,),
        out_shape=(shape((width, TILE), f32), shape((width, total), f32)),
        in_specs=[vmem] * 9,
        out_specs=(
            pl.BlockSpec((TILE, TILE), lambda i: (i, 0)),
            pl.BlockSpec((TILE, total), lambda i: (i, 0)),
        ),
        scratch_shapes=[
            pltpu.VMEM((DEPTH, total), bf16),
            pltpu.VMEM((TILE, total), bf16),
            pltpu.VMEM((TILE, total), bf16),
        ],
        compiler_params=pltpu.CompilerParams(vmem_limit_bytes=48 * 1024 * 1024),
    )(*gathered)


def solution(mesh):
    in_specs = (P("row", None), P("row"), P(), P())
    out_specs = (P("row", None), P("row", "col"))
    return jax.shard_map(shards, mesh=mesh, in_specs=in_specs, out_specs=out_specs, check_vma=False)
```

```python
import functools

import jax
import jax.numpy as jnp
from jax import lax
from jax.experimental import pallas as pl
from jax.experimental.pallas import tpu as pltpu
from jax.sharding import PartitionSpec as P

TILE = 128
FEAT = 64
CAND = 72
DEPTH = 6 * FEAT + 16
BLOCK = 32
HIGHEST = lax.Precision.HIGHEST
MESH = pl.DeviceIdType.MESH
CONTRACT_FIRST = (((0,), (0,)), ((), ()))
CONTRACT_LAST = (((1,), (1,)), ((), ()))


def split3(x):
    hi = x.astype(jnp.bfloat16)
    rest = x - hi.astype(jnp.float32)
    mid = rest.astype(jnp.bfloat16)
    lo = (rest - mid.astype(jnp.float32)).astype(jnp.bfloat16)
    return hi, mid, lo


def norm_rows(f, first):
    sq = jnp.sum(f * f, axis=0, keepdims=True) * (-1.0 / FEAT)
    parts = [p.astype(jnp.float32) for p in split3(sq)]
    row = lax.broadcasted_iota(jnp.int32, (16, f.shape[1]), 0)
    out = jnp.zeros((16, f.shape[1]), jnp.float32)
    for k in range(3):
        out = jnp.where(row == first + k, parts[k], out)
        out = jnp.where(row == 3 - first + k, 1.0, out)
    return out.astype(jnp.bfloat16)


def left_terms(f):
    hi, mid, lo = split3(f * (2.0 / FEAT))
    return jnp.concatenate([hi, hi, mid, mid, hi, lo, norm_rows(f, 0)], axis=0)


def right_terms(f):
    hi, mid, lo = split3(f)
    return jnp.concatenate([hi, mid, hi, mid, lo, hi, norm_rows(f, 3)], axis=0)


def exponent(left, right):
    return lax.dot_general(left, right, CONTRACT_FIRST, preferred_element_type=jnp.float32)


def eliminate(table, between=None):
    lane = lax.broadcasted_iota(jnp.int32, (8, TILE), 1)
    sub = lax.broadcasted_iota(jnp.int32, (8, TILE), 0)
    block_lane = lax.broadcasted_iota(jnp.int32, (BLOCK, TILE), 1)
    block_sub = lax.broadcasted_iota(jnp.int32, (BLOCK, TILE), 0)
    full = (8, TILE)
    done = []
    below = table
    for k in range(TILE // BLOCK):
        groups = [below[g * 8 : g * 8 + 8] for g in range(BLOCK // 8)]
        pieces = []
        for g in range(BLOCK // 8):
            at = k * BLOCK + g * 8
            own = (lane >= at) & (lane < at + 8)
            here = groups[g]
            wide = [jnp.broadcast_to(here[:, at + j : at + j + 1], full) for j in range(8)]
            entry = {
                (i, j): jnp.broadcast_to(wide[j][i : i + 1], full)
                for i in range(8) for j in range(i + 1)
            }
            row = [
                jnp.where(
                    own, jnp.where(lane == at + i, 1.0, 0.0), jnp.broadcast_to(here[i : i + 1], full)
                )
                for i in range(8)
            ]
            later = range(g + 1, BLOCK // 8)
            cols = {
                h: [jnp.broadcast_to(groups[h][:, at + j : at + j + 1], full) for j in range(8)]
                for h in later
            }
            piece = jnp.zeros(full, jnp.float32)
            rest = {h: jnp.where(own, 0.0, groups[h]) for h in later}
            for j in range(8):
                pivot = entry[j, j]
                inv = 1.0 / pivot
                factor = [entry[i, j] * inv for i in range(j + 1, 8)]
                for i in range(j + 1, 8):
                    for l in range(j + 1, i + 1):
                        entry[i, l] = entry[i, l] - factor[i - j - 1] * entry[l, j]
                scaled = row[j] * inv
                for i in range(j + 1, 8):
                    row[i] = row[i] - entry[i, j] * scaled
                piece = jnp.where(sub == j, row[j] / jnp.sqrt(pivot), piece)
                for h in later:
                    for l in range(j + 1, 8):
                        cols[h][l] = cols[h][l] - cols[h][j] * factor[l - j - 1]
                    rest[h] = rest[h] - cols[h][j] * scaled
            for h in later:
                groups[h] = rest[h]
            pieces.append(piece)
            if between is not None:
                between(at // 8)
        block = jnp.concatenate(pieces, axis=0)
        lower = block_lane <= block_sub + k * BLOCK
        done.append(jnp.where(lower, block, 0.0))
        if (k + 1) * BLOCK < TILE:
            own = (lane[:1] >= k * BLOCK) & (lane[:1] < (k + 1) * BLOCK)
            right = jnp.where(lower | (block_lane >= (k + 1) * BLOCK), block, 0.0)
            update = lax.dot_general(
                block, right, CONTRACT_FIRST, precision=HIGHEST, preferred_element_type=jnp.float32
            )
            below = jnp.where(own, 0.0, below[BLOCK:]) - update[(k + 1) * BLOCK :]
    return jnp.concatenate(done, axis=0)


CHUNKS = 4


def gather_kernel(
    lines, across, cols, tiles, map_hbm, panel_ref, feat_hbm, noise_hbm,
    left_out, noise_out, here_out, there_out, pivot_out, inverse_out, pleft_out, pright_out, col_ref,
    map_ref, feat_ref, own_ref, sum_ref, near_ref, far_ref,
    in_sem, near_send, near_recv, far_send, far_recv, line_send, line_recv, side_send, side_recv, local_sem,
):
    r = lax.axis_index("row")
    c = lax.axis_index("col")
    rows = lines * across
    per_col = rows // cols
    z = r // across
    x = lax.rem(r, across)
    loads = [
        pltpu.make_async_copy(src, dst, in_sem.at[n])
        for n, (src, dst) in enumerate(
            [(map_hbm, map_ref), (feat_hbm, feat_ref), (noise_hbm, noise_out)]
        )
    ]
    for load in loads:
        load.start()
    barrier = pltpu.get_barrier_semaphore()
    for d in range(1, rows):
        pl.semaphore_signal(
            barrier, inc=1, device_id={"row": lax.rem(r + d, rows)}, device_id_type=MESH
        )
    for load in loads:
        load.wait()
    pivot_tile = panel_ref[0]
    feat = jnp.zeros((FEAT, TILE), jnp.float32)
    noise = jnp.zeros((1, TILE), jnp.float32)
    for s in range(tiles):
        held = map_ref[r * tiles + s] == pivot_tile
        feat = jnp.where(held, feat_ref[:, s * TILE : (s + 1) * TILE], feat)
        noise = jnp.where(held, noise_out[s : s + 1, :], noise)
    own_ref[:FEAT] = feat
    own_ref[FEAT:] = jnp.broadcast_to(noise, (CAND - FEAT, TILE))
    pl.semaphore_wait(barrier, rows - 1)

    def near(d, src, dst):
        return pltpu.make_async_remote_copy(
            src_ref=own_ref, dst_ref=near_ref.at[d - 1],
            send_sem=near_send.at[d - 1], recv_sem=near_recv.at[d - 1],
            device_id={"row": z * across + lax.rem(x + d, across)}, device_id_type=MESH,
        )

    def far(d):
        return pltpu.make_async_remote_copy(
            src_ref=sum_ref, dst_ref=far_ref.at[d - 1],
            send_sem=far_send.at[d - 1], recv_sem=far_recv.at[d - 1],
            device_id={"row": lax.rem(z + d, lines) * across + x}, device_id_type=MESH,
        )

    nears = [near(d, None, None) for d in range(1, across)]
    fars = [far(d) for d in range(1, lines)]
    for copy in nears:
        copy.start()
    for s in range(tiles):
        left_out[s * TILE : (s + 1) * TILE] = left_terms(feat_ref[:, s * TILE : (s + 1) * TILE]).T
        here_out[s * 8 : s * 8 + 8] = jnp.full((8, TILE), map_ref[r * tiles + s], jnp.int32)
    for t in range(per_col * tiles):
        there_out[:, t * TILE : (t + 1) * TILE] = jnp.full(
            (8, TILE), map_ref[c * per_col * tiles + t], jnp.int32
        )
    pivot_out[...] = jnp.full((8, TILE), pivot_tile, jnp.int32)
    for copy in nears:
        copy.wait_recv()
    total = own_ref[...]
    for d in range(1, across):
        total += near_ref[d - 1]
    sum_ref[...] = total
    for copy in fars:
        copy.start()
    first = c * per_col
    source_z = first // across
    first_x = lax.rem(first, across)
    member = x - first_x
    on_line = (member >= 0) & (member < per_col)
    slot = jnp.clip(member, 0, per_col - 1)
    hop = jnp.abs(z - source_z)
    rows_each = FEAT // CHUNKS

    def chunk(q):
        return col_ref.at[slot, pl.ds(q * rows_each, rows_each)]

    def line_copy(q, side):
        to = jnp.clip(z + (1 if side == 0 else -1), 0, lines - 1)
        return pltpu.make_async_remote_copy(
            src_ref=chunk(q), dst_ref=chunk(q),
            send_sem=line_send.at[side, q], recv_sem=line_recv.at[q],
            device_id={"row": to * across + x}, device_id_type=MESH,
        )

    def side_copy(q, d):
        return pltpu.make_async_remote_copy(
            src_ref=chunk(q), dst_ref=chunk(q),
            send_sem=side_send.at[d - 1, q], recv_sem=side_recv.at[slot, q],
            device_id={"row": z * across + lax.rem(x + d, across)}, device_id_type=MESH,
        )

    up = on_line & (z >= source_z) & (z < lines - 1)
    down = on_line & (z <= source_z) & (z > 0)

    def pass_on(q):
        @pl.when(up)
        def _():
            line_copy(q, 0).start()

        @pl.when(down)
        def _():
            line_copy(q, 1).start()

        for d in range(1, across):
            side_copy(q, d).start()

    def point(p):
        for h in range(lines):
            q = p - 2 * h
            if 0 <= q < CHUNKS:
                @pl.when(on_line & (hop == h))
                def _(h=h, q=q):
                    if h > 0:
                        line_copy(q, 0).wait_recv()
                    pass_on(q)

    @pl.when(on_line & (hop == 0))
    def _():
        own = pltpu.make_async_copy(feat_ref, col_ref.at[slot], local_sem)
        own.start()
        own.wait()

    point(0)
    point(1)
    for copy in fars:
        copy.wait_recv()
    for d in range(1, lines):
        total += far_ref[d - 1]
    pivot = total[:FEAT]
    left = left_terms(pivot)
    right = right_terms(pivot)
    pleft_out[...] = left
    pright_out[...] = right
    eye = lax.broadcasted_iota(jnp.int32, (TILE, TILE), 1) == lax.broadcasted_iota(
        jnp.int32, (TILE, TILE), 0
    )
    table = jnp.exp(exponent(left, right)) + jnp.where(eye, total[FEAT : FEAT + 1], 0.0)
    inverse_out[...] = eliminate(table, lambda n: point(n + 2))
    for p in range(TILE // 8 + 2, CHUNKS + 2 * lines):
        point(p)
    for m in range(per_col):
        for q in range(CHUNKS):
            part = col_ref.at[m, pl.ds(q * rows_each, rows_each)]

            @pl.when(x != first_x + m)
            def _(m=m, q=q, part=part):
                pltpu.make_async_remote_copy(
                    src_ref=part, dst_ref=part, send_sem=side_send.at[0, q],
                    recv_sem=side_recv.at[m, q], device_id={"row": z * across + first_x + m},
                    device_id_type=MESH,
                ).wait_recv()
    for copy in nears + fars:
        copy.wait_send()
    for q in range(CHUNKS):
        @pl.when(up)
        def _(q=q):
            line_copy(q, 0).wait_send()

        @pl.when(down)
        def _(q=q):
            line_copy(q, 1).wait_send()

        @pl.when(on_line)
        def _(q=q):
            for d in range(1, across):
                side_copy(q, d).wait_send()


def panel_kernel(
    tiles, left_ref, noise_ref, here_ref, there_ref, pivot_ref, inverse_ref, pleft_ref,
    pright_ref, col_ref, out_panel, out_trailing, row_terms,
):
    lane = lax.broadcasted_iota(jnp.int32, (TILE, TILE), 1)
    sub = lax.broadcasted_iota(jnp.int32, (TILE, TILE), 0)
    pivot_tile = pivot_ref[0:1, :]
    inverse = inverse_ref[...]

    def tile_of(i):
        here = here_ref[i * 8 : i * 8 + 1, :]
        return here, jnp.where(lane == sub, noise_ref[i : i + 1, :], 0.0)

    @pl.when(pl.program_id(0) == 0)
    def _():
        kern = jnp.exp(jnp.dot(left_ref[...], pright_ref[...], preferred_element_type=jnp.float32))
        parts = []
        for i in range(tiles):
            here, noise = tile_of(i)
            part = kern[i * TILE : (i + 1) * TILE]
            parts.append(part + jnp.where(here == pivot_tile, noise, 0.0))
        panel = lax.dot_general(
            jnp.concatenate(parts, axis=0), inverse, CONTRACT_LAST,
            precision=HIGHEST, preferred_element_type=jnp.float32,
        )
        for i in range(tiles):
            rows = slice(i * TILE, (i + 1) * TILE)
            part = jnp.where(tile_of(i)[0] >= pivot_tile, panel[rows], 0.0)
            out_panel[rows] = part
            hi = part.astype(jnp.bfloat16)
            row_terms[rows, :TILE] = hi
            row_terms[rows, TILE : 2 * TILE] = hi
            row_terms[rows, 2 * TILE :] = (part - hi.astype(jnp.float32)).astype(jnp.bfloat16)

    right = right_terms(col_ref[0])
    kern = jnp.exp(exponent(pleft_ref[...], right))
    panel = jnp.dot(inverse, kern, precision=HIGHEST, preferred_element_type=jnp.float32)
    hi = panel.astype(jnp.bfloat16)
    lo = (panel - hi.astype(jnp.float32)).astype(jnp.bfloat16)
    col_terms = jnp.concatenate([hi, lo, hi], axis=0)
    value = jnp.exp(jnp.dot(left_ref[...], right, preferred_element_type=jnp.float32)) - jnp.dot(
        row_terms[...], col_terms, preferred_element_type=jnp.float32
    )
    for i in range(tiles):
        here, noise = tile_of(i)
        rows = slice(i * TILE, (i + 1) * TILE)
        for u in range(2):
            cols = slice(u * TILE, (u + 1) * TILE)
            there = there_ref[0:1, cols]
            live = (here >= there) & (there > pivot_tile)
            part = value[rows, cols] + jnp.where(here == there, noise, 0.0)
            out_trailing[rows, cols] = jnp.where(live, part, 0.0)


def shards(features, noise, tile_map, panel_tile):
    width = features.shape[0]
    tiles = width // TILE
    rows = lax.axis_size("row")
    cols = lax.axis_size("col")
    per_col = rows // cols
    across = 2 ** ((rows.bit_length() - 1) // 2)
    lines = rows // across
    slots = tile_map.shape[0]
    total = per_col * width
    smem = pl.BlockSpec(memory_space=pltpu.SMEM)
    hbm = pl.BlockSpec(memory_space=pltpu.HBM)
    vmem = pl.BlockSpec(memory_space=pltpu.VMEM)
    dma = pltpu.SemaphoreType.DMA
    f32, bf16, i32 = jnp.float32, jnp.bfloat16, jnp.int32
    shape = jax.ShapeDtypeStruct
    gathered = pl.pallas_call(
        functools.partial(gather_kernel, lines, across, cols, tiles),
        name="gather_and_factor",
        out_shape=(
            shape((width, DEPTH), bf16),
            shape((tiles, TILE), f32),
            shape((tiles * 8, TILE), i32),
            shape((8, total), i32),
            shape((8, TILE), i32),
            shape((TILE, TILE), f32),
            shape((DEPTH, TILE), bf16),
            shape((DEPTH, TILE), bf16),
            shape((per_col, FEAT, width), f32),
        ),
        in_specs=[hbm, smem, hbm, hbm],
        out_specs=(vmem,) * 9,
        scratch_shapes=[
            pltpu.SMEM((slots,), i32),
            pltpu.VMEM((FEAT, width), f32),
            pltpu.VMEM((CAND, TILE), f32),
            pltpu.VMEM((CAND, TILE), f32),
            pltpu.VMEM((across - 1, CAND, TILE), f32),
            pltpu.VMEM((lines - 1, CAND, TILE), f32),
            dma((3,)),
            dma((across - 1,)),
            dma((across - 1,)),
            dma((lines - 1,)),
            dma((lines - 1,)),
            dma((2, CHUNKS)),
            dma((CHUNKS,)),
            dma((across - 1, CHUNKS)),
            dma((per_col, CHUNKS)),
            dma,
        ],
        compiler_params=pltpu.CompilerParams(
            collective_id=0, has_side_effects=True, vmem_limit_bytes=32 * 1024 * 1024
        ),
    )(
        pltpu.with_memory_space_constraint(tile_map, pltpu.HBM),
        panel_tile,
        pltpu.with_memory_space_constraint(features.T, pltpu.HBM),
        pltpu.with_memory_space_constraint(noise.reshape(tiles, TILE), pltpu.HBM),
    )
    step = 2 * TILE
    each = width // step
    return pl.pallas_call(
        functools.partial(panel_kernel, tiles),
        name="panel_and_trailing",
        grid=(per_col * each,),
        out_shape=(shape((width, TILE), f32), shape((width, total), f32)),
        in_specs=[vmem] * 3
        + [pl.BlockSpec((8, step), lambda i: (0, i))]
        + [vmem] * 4
        + [pl.BlockSpec((1, FEAT, step), lambda i: (i // each, 0, i % each))],
        out_specs=(
            pl.BlockSpec((width, TILE), lambda i: (0, 0)),
            pl.BlockSpec((width, step), lambda i: (0, i)),
        ),
        scratch_shapes=[pltpu.VMEM((width, 3 * TILE), bf16)],
        compiler_params=pltpu.CompilerParams(vmem_limit_bytes=48 * 1024 * 1024),
    )(*gathered)


def solution(mesh):
    in_specs = (P("row", None), P("row"), P(), P())
    out_specs = (P("row", None), P("row", "col"))
    return jax.shard_map(shards, mesh=mesh, in_specs=in_specs, out_specs=out_specs, check_vma=False)
```

```python
import functools

import jax
import jax.numpy as jnp
from jax import lax
from jax.experimental import pallas as pl
from jax.experimental.pallas import tpu as pltpu
from jax.sharding import PartitionSpec as P

TILE = 128
FEAT = 64
CAND = 72
DEPTH = 6 * FEAT + 16
BLOCK = 32
HIGHEST = lax.Precision.HIGHEST
MESH = pl.DeviceIdType.MESH
CONTRACT_FIRST = (((0,), (0,)), ((), ()))
CONTRACT_LAST = (((1,), (1,)), ((), ()))


def split3(x):
    hi = x.astype(jnp.bfloat16)
    rest = x - hi.astype(jnp.float32)
    mid = rest.astype(jnp.bfloat16)
    lo = (rest - mid.astype(jnp.float32)).astype(jnp.bfloat16)
    return hi, mid, lo


def norm_rows(f, first):
    sq = jnp.sum(f * f, axis=0, keepdims=True) * (-1.0 / FEAT)
    parts = [p.astype(jnp.float32) for p in split3(sq)]
    row = lax.broadcasted_iota(jnp.int32, (16, f.shape[1]), 0)
    out = jnp.zeros((16, f.shape[1]), jnp.float32)
    for k in range(3):
        out = jnp.where(row == first + k, parts[k], out)
        out = jnp.where(row == 3 - first + k, 1.0, out)
    return out.astype(jnp.bfloat16)


def left_terms(f):
    hi, mid, lo = split3(f * (2.0 / FEAT))
    return jnp.concatenate([hi, hi, mid, mid, hi, lo, norm_rows(f, 0)], axis=0)


def right_terms(f):
    hi, mid, lo = split3(f)
    return jnp.concatenate([hi, mid, hi, mid, lo, hi, norm_rows(f, 3)], axis=0)


def exponent(left, right):
    return lax.dot_general(left, right, CONTRACT_FIRST, preferred_element_type=jnp.float32)


def eliminate(table, between=None):
    lane = lax.broadcasted_iota(jnp.int32, (8, TILE), 1)
    sub = lax.broadcasted_iota(jnp.int32, (8, TILE), 0)
    block_lane = lax.broadcasted_iota(jnp.int32, (BLOCK, TILE), 1)
    block_sub = lax.broadcasted_iota(jnp.int32, (BLOCK, TILE), 0)
    full = (8, TILE)
    done = []
    below = table
    for k in range(TILE // BLOCK):
        groups = [below[g * 8 : g * 8 + 8] for g in range(BLOCK // 8)]
        pieces = []
        for g in range(BLOCK // 8):
            at = k * BLOCK + g * 8
            own = (lane >= at) & (lane < at + 8)
            here = groups[g]
            wide = [jnp.broadcast_to(here[:, at + j : at + j + 1], full) for j in range(8)]
            entry = {
                (i, j): jnp.broadcast_to(wide[j][i : i + 1], full)
                for i in range(8) for j in range(i + 1)
            }
            row = [
                jnp.where(
                    own, jnp.where(lane == at + i, 1.0, 0.0), jnp.broadcast_to(here[i : i + 1], full)
                )
                for i in range(8)
            ]
            later = range(g + 1, BLOCK // 8)
            cols = {
                h: [jnp.broadcast_to(groups[h][:, at + j : at + j + 1], full) for j in range(8)]
                for h in later
            }
            piece = jnp.zeros(full, jnp.float32)
            rest = {h: jnp.where(own, 0.0, groups[h]) for h in later}
            for j in range(8):
                pivot = entry[j, j]
                inv = 1.0 / pivot
                factor = [entry[i, j] * inv for i in range(j + 1, 8)]
                for i in range(j + 1, 8):
                    for l in range(j + 1, i + 1):
                        entry[i, l] = entry[i, l] - factor[i - j - 1] * entry[l, j]
                scaled = row[j] * inv
                for i in range(j + 1, 8):
                    row[i] = row[i] - entry[i, j] * scaled
                piece = jnp.where(sub == j, row[j] / jnp.sqrt(pivot), piece)
                for h in later:
                    for l in range(j + 1, 8):
                        cols[h][l] = cols[h][l] - cols[h][j] * factor[l - j - 1]
                    rest[h] = rest[h] - cols[h][j] * scaled
            for h in later:
                groups[h] = rest[h]
            pieces.append(piece)
            if between is not None:
                between(at // 8)
        block = jnp.concatenate(pieces, axis=0)
        lower = block_lane <= block_sub + k * BLOCK
        done.append(jnp.where(lower, block, 0.0))
        if (k + 1) * BLOCK < TILE:
            own = (lane[:1] >= k * BLOCK) & (lane[:1] < (k + 1) * BLOCK)
            right = jnp.where(lower | (block_lane >= (k + 1) * BLOCK), block, 0.0)
            update = lax.dot_general(
                block, right, CONTRACT_FIRST, precision=HIGHEST, preferred_element_type=jnp.float32
            )
            below = jnp.where(own, 0.0, below[BLOCK:]) - update[(k + 1) * BLOCK :]
    return jnp.concatenate(done, axis=0)


CHUNKS = 4


def gather_kernel(
    lines, across, cols, tiles, map_hbm, panel_ref, feat_hbm, noise_hbm,
    left_out, noise_out, here_out, there_out, pivot_out, inverse_out, pleft_out, kern_out, col_ref,
    map_ref, feat_ref, own_ref, sum_ref, near_ref, far_ref,
    in_sem, near_send, near_recv, far_send, far_recv, line_send, line_recv, side_send, side_recv, local_sem,
):
    r = lax.axis_index("row")
    c = lax.axis_index("col")
    rows = lines * across
    per_col = rows // cols
    z = r // across
    x = lax.rem(r, across)
    loads = [
        pltpu.make_async_copy(src, dst, in_sem.at[n])
        for n, (src, dst) in enumerate(
            [(map_hbm, map_ref), (feat_hbm, feat_ref), (noise_hbm, noise_out)]
        )
    ]
    for load in loads:
        load.start()
    barrier = pltpu.get_barrier_semaphore()
    for d in range(1, rows):
        pl.semaphore_signal(
            barrier, inc=1, device_id={"row": lax.rem(r + d, rows)}, device_id_type=MESH
        )
    for load in loads:
        load.wait()
    pivot_tile = panel_ref[0]
    feat = jnp.zeros((FEAT, TILE), jnp.float32)
    noise = jnp.zeros((1, TILE), jnp.float32)
    for s in range(tiles):
        held = map_ref[r * tiles + s] == pivot_tile
        feat = jnp.where(held, feat_ref[:, s * TILE : (s + 1) * TILE], feat)
        noise = jnp.where(held, noise_out[s : s + 1, :], noise)
    own_ref[:FEAT] = feat
    own_ref[FEAT:] = jnp.broadcast_to(noise, (CAND - FEAT, TILE))
    pl.semaphore_wait(barrier, rows - 1)

    def near(d, src, dst):
        return pltpu.make_async_remote_copy(
            src_ref=own_ref, dst_ref=near_ref.at[d - 1],
            send_sem=near_send.at[d - 1], recv_sem=near_recv.at[d - 1],
            device_id={"row": z * across + lax.rem(x + d, across)}, device_id_type=MESH,
        )

    def far(d):
        return pltpu.make_async_remote_copy(
            src_ref=sum_ref, dst_ref=far_ref.at[d - 1],
            send_sem=far_send.at[d - 1], recv_sem=far_recv.at[d - 1],
            device_id={"row": lax.rem(z + d, lines) * across + x}, device_id_type=MESH,
        )

    nears = [near(d, None, None) for d in range(1, across)]
    fars = [far(d) for d in range(1, lines)]
    for copy in nears:
        copy.start()
    for copy in nears:
        copy.wait_recv()
    total = own_ref[...]
    for d in range(1, across):
        total += near_ref[d - 1]
    sum_ref[...] = total
    for copy in fars:
        copy.start()
    first = c * per_col
    source_z = first // across
    first_x = lax.rem(first, across)
    member = x - first_x
    on_line = (member >= 0) & (member < per_col)
    slot = jnp.clip(member, 0, per_col - 1)
    hop = jnp.abs(z - source_z)
    rows_each = FEAT // CHUNKS

    def chunk(q):
        return col_ref.at[slot, pl.ds(q * rows_each, rows_each)]

    def line_copy(q, side):
        to = jnp.clip(z + (1 if side == 0 else -1), 0, lines - 1)
        return pltpu.make_async_remote_copy(
            src_ref=chunk(q), dst_ref=chunk(q),
            send_sem=line_send.at[side, q], recv_sem=line_recv.at[q],
            device_id={"row": to * across + x}, device_id_type=MESH,
        )

    def side_copy(q, d):
        return pltpu.make_async_remote_copy(
            src_ref=chunk(q), dst_ref=chunk(q),
            send_sem=side_send.at[d - 1, q], recv_sem=side_recv.at[slot, q],
            device_id={"row": z * across + lax.rem(x + d, across)}, device_id_type=MESH,
        )

    up = on_line & (z >= source_z) & (z < lines - 1)
    down = on_line & (z <= source_z) & (z > 0)

    def pass_on(q):
        @pl.when(up)
        def _():
            line_copy(q, 0).start()

        @pl.when(down)
        def _():
            line_copy(q, 1).start()

        for d in range(1, across):
            side_copy(q, d).start()

    def point(p):
        for h in range(lines):
            q = p - 2 * h
            if 0 <= q < CHUNKS:
                @pl.when(on_line & (hop == h))
                def _(h=h, q=q):
                    if h > 0:
                        line_copy(q, 0).wait_recv()
                    pass_on(q)

    @pl.when(on_line & (hop == 0))
    def _():
        own = pltpu.make_async_copy(feat_ref, col_ref.at[slot], local_sem)
        own.start()
        own.wait()

    point(0)
    point(1)
    for copy in fars:
        copy.wait_recv()
    for d in range(1, lines):
        total += far_ref[d - 1]
    pivot = total[:FEAT]
    left = left_terms(pivot)
    right = right_terms(pivot)
    pleft_out[...] = left
    eye = lax.broadcasted_iota(jnp.int32, (TILE, TILE), 1) == lax.broadcasted_iota(
        jnp.int32, (TILE, TILE), 0
    )
    table = jnp.exp(exponent(left, right)) + jnp.where(eye, total[FEAT : FEAT + 1], 0.0)

    def beside(n):
        if n < tiles:
            rows = slice(n * TILE, (n + 1) * TILE)
            left_out[rows] = left_terms(feat_ref[:, rows]).T
            here_out[n * 8 : n * 8 + 8] = jnp.full((8, TILE), map_ref[r * tiles + n], jnp.int32)
        elif n < 2 * tiles:
            s = n - tiles
            rows = slice(s * TILE, (s + 1) * TILE)
            kern = jnp.exp(jnp.dot(left_out[rows], right, preferred_element_type=jnp.float32))
            held = map_ref[r * tiles + s] == pivot_tile
            kern_out[rows] = kern + jnp.where(eye & held, noise_out[s : s + 1], 0.0)
        elif n == 2 * tiles:
            for t in range(per_col * tiles):
                there_out[:, t * TILE : (t + 1) * TILE] = jnp.full(
                    (8, TILE), map_ref[c * per_col * tiles + t], jnp.int32
                )
            pivot_out[...] = jnp.full((8, TILE), pivot_tile, jnp.int32)
        point(n + 2)

    inverse_out[...] = eliminate(table, beside)
    for p in range(TILE // 8 + 2, CHUNKS + 2 * lines):
        point(p)
    for m in range(per_col):
        for q in range(CHUNKS):
            part = col_ref.at[m, pl.ds(q * rows_each, rows_each)]

            @pl.when(x != first_x + m)
            def _(m=m, q=q, part=part):
                pltpu.make_async_remote_copy(
                    src_ref=part, dst_ref=part, send_sem=side_send.at[0, q],
                    recv_sem=side_recv.at[m, q], device_id={"row": z * across + first_x + m},
                    device_id_type=MESH,
                ).wait_recv()
    for copy in nears + fars:
        copy.wait_send()
    for q in range(CHUNKS):
        @pl.when(up)
        def _(q=q):
            line_copy(q, 0).wait_send()

        @pl.when(down)
        def _(q=q):
            line_copy(q, 1).wait_send()

        @pl.when(on_line)
        def _(q=q):
            for d in range(1, across):
                side_copy(q, d).wait_send()


def panel_kernel(
    tiles, left_ref, noise_ref, here_ref, there_ref, pivot_ref, inverse_ref, pleft_ref,
    kern_ref, col_ref, out_panel, out_trailing, row_terms, right_ref, col_terms,
):
    lane = lax.broadcasted_iota(jnp.int32, (TILE, TILE), 1)
    sub = lax.broadcasted_iota(jnp.int32, (TILE, TILE), 0)
    pivot_tile = pivot_ref[0:1, :]
    inverse = inverse_ref[...]

    def tile_of(i):
        here = here_ref[i * 8 : i * 8 + 1, :]
        return here, jnp.where(lane == sub, noise_ref[i : i + 1, :], 0.0)

    @pl.when(pl.program_id(0) == 0)
    def _():
        panel = lax.dot_general(
            kern_ref[...], inverse, CONTRACT_LAST,
            precision=HIGHEST, preferred_element_type=jnp.float32,
        )
        for i in range(tiles):
            rows = slice(i * TILE, (i + 1) * TILE)
            part = jnp.where(tile_of(i)[0] >= pivot_tile, panel[rows], 0.0)
            out_panel[rows] = part
            hi = part.astype(jnp.bfloat16)
            row_terms[rows, :TILE] = hi
            row_terms[rows, TILE : 2 * TILE] = hi
            row_terms[rows, 2 * TILE :] = (part - hi.astype(jnp.float32)).astype(jnp.bfloat16)

        for m in range(col_ref.shape[0]):
            right = right_terms(col_ref[m])
            cols = slice(m * tiles * TILE, (m + 1) * tiles * TILE)
            right_ref[:, cols] = right
            kern = jnp.exp(exponent(pleft_ref[...], right))
            part = jnp.dot(inverse, kern, precision=HIGHEST, preferred_element_type=jnp.float32)
            hi = part.astype(jnp.bfloat16)
            col_terms[:TILE, cols] = hi
            col_terms[TILE : 2 * TILE, cols] = (part - hi.astype(jnp.float32)).astype(jnp.bfloat16)
            col_terms[2 * TILE :, cols] = hi

    step = out_trailing.shape[1]
    now = pl.ds(pl.multiple_of(pl.program_id(0) * step, step), step)
    value = jnp.exp(
        jnp.dot(left_ref[...], right_ref[:, now], preferred_element_type=jnp.float32)
    ) - jnp.dot(row_terms[...], col_terms[:, now], preferred_element_type=jnp.float32)
    for i in range(tiles):
        here, noise = tile_of(i)
        rows = slice(i * TILE, (i + 1) * TILE)
        for u in range(2):
            cols = slice(u * TILE, (u + 1) * TILE)
            there = there_ref[0:1, cols]
            live = (here >= there) & (there > pivot_tile)
            part = value[rows, cols] + jnp.where(here == there, noise, 0.0)
            out_trailing[rows, cols] = jnp.where(live, part, 0.0)


def shards(features, noise, tile_map, panel_tile):
    width = features.shape[0]
    tiles = width // TILE
    rows = lax.axis_size("row")
    cols = lax.axis_size("col")
    per_col = rows // cols
    across = 2 ** ((rows.bit_length() - 1) // 2)
    lines = rows // across
    slots = tile_map.shape[0]
    total = per_col * width
    smem = pl.BlockSpec(memory_space=pltpu.SMEM)
    hbm = pl.BlockSpec(memory_space=pltpu.HBM)
    vmem = pl.BlockSpec(memory_space=pltpu.VMEM)
    dma = pltpu.SemaphoreType.DMA
    f32, bf16, i32 = jnp.float32, jnp.bfloat16, jnp.int32
    shape = jax.ShapeDtypeStruct
    gathered = pl.pallas_call(
        functools.partial(gather_kernel, lines, across, cols, tiles),
        name="gather_and_factor",
        out_shape=(
            shape((width, DEPTH), bf16),
            shape((tiles, TILE), f32),
            shape((tiles * 8, TILE), i32),
            shape((8, total), i32),
            shape((8, TILE), i32),
            shape((TILE, TILE), f32),
            shape((DEPTH, TILE), bf16),
            shape((width, TILE), f32),
            shape((per_col, FEAT, width), f32),
        ),
        in_specs=[hbm, smem, hbm, hbm],
        out_specs=(vmem,) * 9,
        scratch_shapes=[
            pltpu.SMEM((slots,), i32),
            pltpu.VMEM((FEAT, width), f32),
            pltpu.VMEM((CAND, TILE), f32),
            pltpu.VMEM((CAND, TILE), f32),
            pltpu.VMEM((across - 1, CAND, TILE), f32),
            pltpu.VMEM((lines - 1, CAND, TILE), f32),
            dma((3,)),
            dma((across - 1,)),
            dma((across - 1,)),
            dma((lines - 1,)),
            dma((lines - 1,)),
            dma((2, CHUNKS)),
            dma((CHUNKS,)),
            dma((across - 1, CHUNKS)),
            dma((per_col, CHUNKS)),
            dma,
        ],
        compiler_params=pltpu.CompilerParams(
            collective_id=0, has_side_effects=True, vmem_limit_bytes=32 * 1024 * 1024
        ),
    )(
        pltpu.with_memory_space_constraint(tile_map, pltpu.HBM),
        panel_tile,
        pltpu.with_memory_space_constraint(features.T, pltpu.HBM),
        pltpu.with_memory_space_constraint(noise.reshape(tiles, TILE), pltpu.HBM),
    )
    step = 2 * TILE
    return pl.pallas_call(
        functools.partial(panel_kernel, tiles),
        name="panel_and_trailing",
        grid=(total // step,),
        out_shape=(shape((width, TILE), f32), shape((width, total), f32)),
        in_specs=[vmem] * 3
        + [pl.BlockSpec((8, step), lambda i: (0, i))]
        + [vmem] * 5,
        out_specs=(
            pl.BlockSpec((width, TILE), lambda i: (0, 0)),
            pl.BlockSpec((width, step), lambda i: (0, i)),
        ),
        scratch_shapes=[
            pltpu.VMEM((width, 3 * TILE), bf16),
            pltpu.VMEM((DEPTH, total), bf16),
            pltpu.VMEM((3 * TILE, total), bf16),
        ],
        compiler_params=pltpu.CompilerParams(vmem_limit_bytes=48 * 1024 * 1024),
    )(*gathered)


def solution(mesh):
    in_specs = (P("row", None), P("row"), P(), P())
    out_specs = (P("row", None), P("row", "col"))
    return jax.shard_map(shards, mesh=mesh, in_specs=in_specs, out_specs=out_specs, check_vma=False)
```

```python
import functools

import jax
import jax.numpy as jnp
from jax import lax
from jax.experimental import pallas as pl
from jax.experimental.pallas import tpu as pltpu
from jax.sharding import PartitionSpec as P

TILE = 128
FEAT = 64
CAND = 72
DEPTH = 6 * FEAT + 16
BLOCK = 32
HIGHEST = lax.Precision.HIGHEST
MESH = pl.DeviceIdType.MESH
CONTRACT_FIRST = (((0,), (0,)), ((), ()))
CONTRACT_LAST = (((1,), (1,)), ((), ()))


def split3(x):
    hi = x.astype(jnp.bfloat16)
    rest = x - hi.astype(jnp.float32)
    mid = rest.astype(jnp.bfloat16)
    lo = (rest - mid.astype(jnp.float32)).astype(jnp.bfloat16)
    return hi, mid, lo


def norm_rows(f, first):
    sq = jnp.sum(f * f, axis=0, keepdims=True) * (-1.0 / FEAT)
    parts = [p.astype(jnp.float32) for p in split3(sq)]
    row = lax.broadcasted_iota(jnp.int32, (16, f.shape[1]), 0)
    out = jnp.zeros((16, f.shape[1]), jnp.float32)
    for k in range(3):
        out = jnp.where(row == first + k, parts[k], out)
        out = jnp.where(row == 3 - first + k, 1.0, out)
    return out.astype(jnp.bfloat16)


def left_terms(f):
    hi, mid, lo = split3(f * (2.0 / FEAT))
    return jnp.concatenate([hi, hi, mid, mid, hi, lo, norm_rows(f, 0)], axis=0)


def right_terms(f):
    hi, mid, lo = split3(f)
    return jnp.concatenate([hi, mid, hi, mid, lo, hi, norm_rows(f, 3)], axis=0)


def exponent(left, right):
    return lax.dot_general(left, right, CONTRACT_FIRST, preferred_element_type=jnp.float32)


def eliminate(table, between=None):
    lane = lax.broadcasted_iota(jnp.int32, (8, TILE), 1)
    sub = lax.broadcasted_iota(jnp.int32, (8, TILE), 0)
    block_lane = lax.broadcasted_iota(jnp.int32, (BLOCK, TILE), 1)
    block_sub = lax.broadcasted_iota(jnp.int32, (BLOCK, TILE), 0)
    full = (8, TILE)
    done = []
    below = table
    for k in range(TILE // BLOCK):
        groups = [below[g * 8 : g * 8 + 8] for g in range(BLOCK // 8)]
        pieces = []
        for g in range(BLOCK // 8):
            at = k * BLOCK + g * 8
            own = (lane >= at) & (lane < at + 8)
            here = groups[g]
            wide = [jnp.broadcast_to(here[:, at + j : at + j + 1], full) for j in range(8)]
            entry = {
                (i, j): jnp.broadcast_to(wide[j][i : i + 1], full)
                for i in range(8) for j in range(i + 1)
            }
            row = [
                jnp.where(
                    own, jnp.where(lane == at + i, 1.0, 0.0), jnp.broadcast_to(here[i : i + 1], full)
                )
                for i in range(8)
            ]
            later = range(g + 1, BLOCK // 8)
            cols = {
                h: [jnp.broadcast_to(groups[h][:, at + j : at + j + 1], full) for j in range(8)]
                for h in later
            }
            piece = jnp.zeros(full, jnp.float32)
            rest = {h: jnp.where(own, 0.0, groups[h]) for h in later}
            for j in range(8):
                pivot = entry[j, j]
                inv = 1.0 / pivot
                factor = [entry[i, j] * inv for i in range(j + 1, 8)]
                for i in range(j + 1, 8):
                    for l in range(j + 1, i + 1):
                        entry[i, l] = entry[i, l] - factor[i - j - 1] * entry[l, j]
                scaled = row[j] * inv
                for i in range(j + 1, 8):
                    row[i] = row[i] - entry[i, j] * scaled
                piece = jnp.where(sub == j, row[j] / jnp.sqrt(pivot), piece)
                for h in later:
                    for l in range(j + 1, 8):
                        cols[h][l] = cols[h][l] - cols[h][j] * factor[l - j - 1]
                    rest[h] = rest[h] - cols[h][j] * scaled
            for h in later:
                groups[h] = rest[h]
            pieces.append(piece)
            if between is not None:
                between(at // 8)
        block = jnp.concatenate(pieces, axis=0)
        lower = block_lane <= block_sub + k * BLOCK
        done.append(jnp.where(lower, block, 0.0))
        if (k + 1) * BLOCK < TILE:
            own = (lane[:1] >= k * BLOCK) & (lane[:1] < (k + 1) * BLOCK)
            right = jnp.where(lower | (block_lane >= (k + 1) * BLOCK), block, 0.0)
            update = lax.dot_general(
                block, right, CONTRACT_FIRST, precision=HIGHEST, preferred_element_type=jnp.float32
            )
            below = jnp.where(own, 0.0, below[BLOCK:]) - update[(k + 1) * BLOCK :]
    return jnp.concatenate(done, axis=0)


CHUNKS = 4
LAG = 4


def gather_kernel(
    lines, across, cols, tiles, map_hbm, panel_ref, feat_hbm, noise_hbm,
    left_out, noise_out, here_out, there_out, pivot_out, inverse_out, pleft_out, kern_out, col_ref,
    map_ref, feat_ref, own_ref, sum_ref, near_ref, far_ref,
    in_sem, near_send, near_recv, far_send, far_recv, line_send, line_recv, side_send, side_recv, local_sem,
):
    r = lax.axis_index("row")
    c = lax.axis_index("col")
    rows = lines * across
    per_col = rows // cols
    z = r // across
    x = lax.rem(r, across)
    loads = [
        pltpu.make_async_copy(src, dst, in_sem.at[n])
        for n, (src, dst) in enumerate(
            [(map_hbm, map_ref), (feat_hbm, feat_ref), (noise_hbm, noise_out)]
        )
    ]
    for load in loads:
        load.start()
    barrier = pltpu.get_barrier_semaphore()
    for d in range(1, rows):
        pl.semaphore_signal(
            barrier, inc=1, device_id={"row": lax.rem(r + d, rows)}, device_id_type=MESH
        )
    for load in loads:
        load.wait()
    pivot_tile = panel_ref[0]
    feat = jnp.zeros((FEAT, TILE), jnp.float32)
    noise = jnp.zeros((1, TILE), jnp.float32)
    for s in range(tiles):
        held = map_ref[r * tiles + s] == pivot_tile
        feat = jnp.where(held, feat_ref[:, s * TILE : (s + 1) * TILE], feat)
        noise = jnp.where(held, noise_out[s : s + 1, :], noise)
    own_ref[:FEAT] = feat
    own_ref[FEAT:] = jnp.broadcast_to(noise, (CAND - FEAT, TILE))
    pl.semaphore_wait(barrier, rows - 1)

    def near(d, src, dst):
        return pltpu.make_async_remote_copy(
            src_ref=own_ref, dst_ref=near_ref.at[d - 1],
            send_sem=near_send.at[d - 1], recv_sem=near_recv.at[d - 1],
            device_id={"row": z * across + lax.rem(x + d, across)}, device_id_type=MESH,
        )

    def far(d):
        return pltpu.make_async_remote_copy(
            src_ref=sum_ref, dst_ref=far_ref.at[d - 1],
            send_sem=far_send.at[d - 1], recv_sem=far_recv.at[d - 1],
            device_id={"row": lax.rem(z + d, lines) * across + x}, device_id_type=MESH,
        )

    nears = [near(d, None, None) for d in range(1, across)]
    fars = [far(d) for d in range(1, lines)]
    for copy in nears:
        copy.start()
    for copy in nears:
        copy.wait_recv()
    total = own_ref[...]
    for d in range(1, across):
        total += near_ref[d - 1]
    sum_ref[...] = total
    for copy in fars:
        copy.start()
    first = c * per_col
    source_z = first // across
    first_x = lax.rem(first, across)
    member = x - first_x
    on_line = (member >= 0) & (member < per_col)
    slot = jnp.clip(member, 0, per_col - 1)
    hop = jnp.abs(z - source_z)
    rows_each = FEAT // CHUNKS

    def chunk(q):
        return col_ref.at[slot, pl.ds(q * rows_each, rows_each)]

    def line_copy(q, side):
        to = jnp.clip(z + (1 if side == 0 else -1), 0, lines - 1)
        return pltpu.make_async_remote_copy(
            src_ref=chunk(q), dst_ref=chunk(q),
            send_sem=line_send.at[side, q], recv_sem=line_recv.at[q],
            device_id={"row": to * across + x}, device_id_type=MESH,
        )

    def side_copy(q, d):
        return pltpu.make_async_remote_copy(
            src_ref=chunk(q), dst_ref=chunk(q),
            send_sem=side_send.at[d - 1, q], recv_sem=side_recv.at[slot, q],
            device_id={"row": z * across + lax.rem(x + d, across)}, device_id_type=MESH,
        )

    up = on_line & (z >= source_z) & (z < lines - 1)
    down = on_line & (z <= source_z) & (z > 0)

    def pass_on(q):
        @pl.when(up)
        def _():
            line_copy(q, 0).start()

        @pl.when(down)
        def _():
            line_copy(q, 1).start()

        for d in range(1, across):
            side_copy(q, d).start()

    def point(p):
        for h in range(lines):
            q = p - LAG * h
            if 0 <= q < CHUNKS:
                @pl.when(on_line & (hop == h))
                def _(h=h, q=q):
                    if h > 0:
                        line_copy(q, 0).wait_recv()
                    pass_on(q)

    @pl.when(on_line & (hop == 0))
    def _():
        own = pltpu.make_async_copy(feat_ref, col_ref.at[slot], local_sem)
        own.start()
        own.wait()

    for p in range(LAG):
        point(p)
    for copy in fars:
        copy.wait_recv()
    for d in range(1, lines):
        total += far_ref[d - 1]
    pivot = total[:FEAT]
    left = left_terms(pivot)
    right = right_terms(pivot)
    pleft_out[...] = left
    eye = lax.broadcasted_iota(jnp.int32, (TILE, TILE), 1) == lax.broadcasted_iota(
        jnp.int32, (TILE, TILE), 0
    )
    table = jnp.exp(exponent(left, right)) + jnp.where(eye, total[FEAT : FEAT + 1], 0.0)

    def beside(n):
        if n < tiles:
            rows = slice(n * TILE, (n + 1) * TILE)
            left_out[rows] = left_terms(feat_ref[:, rows]).T
            here_out[n * 8 : n * 8 + 8] = jnp.full((8, TILE), map_ref[r * tiles + n], jnp.int32)
        elif n < 2 * tiles:
            s = n - tiles
            rows = slice(s * TILE, (s + 1) * TILE)
            kern = jnp.exp(jnp.dot(left_out[rows], right, preferred_element_type=jnp.float32))
            held = map_ref[r * tiles + s] == pivot_tile
            kern_out[rows] = kern + jnp.where(eye & held, noise_out[s : s + 1], 0.0)
        elif n == 2 * tiles:
            for t in range(per_col * tiles):
                there_out[:, t * TILE : (t + 1) * TILE] = jnp.full(
                    (8, TILE), map_ref[c * per_col * tiles + t], jnp.int32
                )
            pivot_out[...] = jnp.full((8, TILE), pivot_tile, jnp.int32)
        point(n + LAG)

    inverse_out[...] = eliminate(table, beside)
    for p in range(TILE // 8 + LAG, CHUNKS + LAG * lines):
        point(p)
    for m in range(per_col):
        for q in range(CHUNKS):
            part = col_ref.at[m, pl.ds(q * rows_each, rows_each)]

            @pl.when(x != first_x + m)
            def _(m=m, q=q, part=part):
                pltpu.make_async_remote_copy(
                    src_ref=part, dst_ref=part, send_sem=side_send.at[0, q],
                    recv_sem=side_recv.at[m, q], device_id={"row": z * across + first_x + m},
                    device_id_type=MESH,
                ).wait_recv()
    for copy in nears + fars:
        copy.wait_send()
    for q in range(CHUNKS):
        @pl.when(up)
        def _(q=q):
            line_copy(q, 0).wait_send()

        @pl.when(down)
        def _(q=q):
            line_copy(q, 1).wait_send()

        @pl.when(on_line)
        def _(q=q):
            for d in range(1, across):
                side_copy(q, d).wait_send()


def panel_kernel(
    tiles, left_ref, noise_ref, here_ref, there_ref, pivot_ref, inverse_ref, pleft_ref,
    kern_ref, col_ref, out_panel, out_trailing, row_terms, right_ref, col_terms,
):
    lane = lax.broadcasted_iota(jnp.int32, (TILE, TILE), 1)
    sub = lax.broadcasted_iota(jnp.int32, (TILE, TILE), 0)
    pivot_tile = pivot_ref[0:1, :]
    inverse = inverse_ref[...]

    def tile_of(i):
        here = here_ref[i * 8 : i * 8 + 1, :]
        return here, jnp.where(lane == sub, noise_ref[i : i + 1, :], 0.0)

    @pl.when(pl.program_id(0) == 0)
    def _():
        panel = lax.dot_general(
            kern_ref[...], inverse, CONTRACT_LAST,
            precision=HIGHEST, preferred_element_type=jnp.float32,
        )
        for i in range(tiles):
            rows = slice(i * TILE, (i + 1) * TILE)
            part = jnp.where(tile_of(i)[0] >= pivot_tile, panel[rows], 0.0)
            out_panel[rows] = part
            hi = part.astype(jnp.bfloat16)
            row_terms[rows, :TILE] = hi
            row_terms[rows, TILE : 2 * TILE] = hi
            row_terms[rows, 2 * TILE :] = (part - hi.astype(jnp.float32)).astype(jnp.bfloat16)

        for m in range(col_ref.shape[0]):
            right = right_terms(col_ref[m])
            cols = slice(m * tiles * TILE, (m + 1) * tiles * TILE)
            right_ref[:, cols] = right
            kern = jnp.exp(exponent(pleft_ref[...], right))
            part = jnp.dot(inverse, kern, precision=HIGHEST, preferred_element_type=jnp.float32)
            hi = part.astype(jnp.bfloat16)
            col_terms[:TILE, cols] = hi
            col_terms[TILE : 2 * TILE, cols] = (part - hi.astype(jnp.float32)).astype(jnp.bfloat16)
            col_terms[2 * TILE :, cols] = hi

    step = out_trailing.shape[1]
    now = pl.ds(pl.multiple_of(pl.program_id(0) * step, step), step)
    value = jnp.exp(
        jnp.dot(left_ref[...], right_ref[:, now], preferred_element_type=jnp.float32)
    ) - jnp.dot(row_terms[...], col_terms[:, now], preferred_element_type=jnp.float32)
    for i in range(tiles):
        here, noise = tile_of(i)
        rows = slice(i * TILE, (i + 1) * TILE)
        for u in range(2):
            cols = slice(u * TILE, (u + 1) * TILE)
            there = there_ref[0:1, cols]
            live = (here >= there) & (there > pivot_tile)
            part = value[rows, cols] + jnp.where(here == there, noise, 0.0)
            out_trailing[rows, cols] = jnp.where(live, part, 0.0)


def shards(features, noise, tile_map, panel_tile):
    width = features.shape[0]
    tiles = width // TILE
    rows = lax.axis_size("row")
    cols = lax.axis_size("col")
    per_col = rows // cols
    across = 2 ** ((rows.bit_length() - 1) // 2)
    lines = rows // across
    slots = tile_map.shape[0]
    total = per_col * width
    smem = pl.BlockSpec(memory_space=pltpu.SMEM)
    hbm = pl.BlockSpec(memory_space=pltpu.HBM)
    vmem = pl.BlockSpec(memory_space=pltpu.VMEM)
    dma = pltpu.SemaphoreType.DMA
    f32, bf16, i32 = jnp.float32, jnp.bfloat16, jnp.int32
    shape = jax.ShapeDtypeStruct
    gathered = pl.pallas_call(
        functools.partial(gather_kernel, lines, across, cols, tiles),
        name="gather_and_factor",
        out_shape=(
            shape((width, DEPTH), bf16),
            shape((tiles, TILE), f32),
            shape((tiles * 8, TILE), i32),
            shape((8, total), i32),
            shape((8, TILE), i32),
            shape((TILE, TILE), f32),
            shape((DEPTH, TILE), bf16),
            shape((width, TILE), f32),
            shape((per_col, FEAT, width), f32),
        ),
        in_specs=[hbm, smem, hbm, hbm],
        out_specs=(vmem,) * 9,
        scratch_shapes=[
            pltpu.SMEM((slots,), i32),
            pltpu.VMEM((FEAT, width), f32),
            pltpu.VMEM((CAND, TILE), f32),
            pltpu.VMEM((CAND, TILE), f32),
            pltpu.VMEM((across - 1, CAND, TILE), f32),
            pltpu.VMEM((lines - 1, CAND, TILE), f32),
            dma((3,)),
            dma((across - 1,)),
            dma((across - 1,)),
            dma((lines - 1,)),
            dma((lines - 1,)),
            dma((2, CHUNKS)),
            dma((CHUNKS,)),
            dma((across - 1, CHUNKS)),
            dma((per_col, CHUNKS)),
            dma,
        ],
        compiler_params=pltpu.CompilerParams(
            collective_id=0, has_side_effects=True, vmem_limit_bytes=32 * 1024 * 1024
        ),
    )(
        pltpu.with_memory_space_constraint(tile_map, pltpu.HBM),
        panel_tile,
        pltpu.with_memory_space_constraint(features.T, pltpu.HBM),
        pltpu.with_memory_space_constraint(noise.reshape(tiles, TILE), pltpu.HBM),
    )
    step = 2 * TILE
    return pl.pallas_call(
        functools.partial(panel_kernel, tiles),
        name="panel_and_trailing",
        grid=(total // step,),
        out_shape=(shape((width, TILE), f32), shape((width, total), f32)),
        in_specs=[vmem] * 3
        + [pl.BlockSpec((8, step), lambda i: (0, i))]
        + [vmem] * 5,
        out_specs=(
            pl.BlockSpec((width, TILE), lambda i: (0, 0)),
            pl.BlockSpec((width, step), lambda i: (0, i)),
        ),
        scratch_shapes=[
            pltpu.VMEM((width, 3 * TILE), bf16),
            pltpu.VMEM((DEPTH, total), bf16),
            pltpu.VMEM((3 * TILE, total), bf16),
        ],
        compiler_params=pltpu.CompilerParams(vmem_limit_bytes=48 * 1024 * 1024),
    )(*gathered)


def solution(mesh):
    in_specs = (P("row", None), P("row"), P(), P())
    out_specs = (P("row", None), P("row", "col"))
    return jax.shard_map(shards, mesh=mesh, in_specs=in_specs, out_specs=out_specs, check_vma=False)
```
